32 devices in a mesh: own: 4 (over x, core), seq: 2 (over y), tp: 4 (over z).
Axes of the slice: x: 2, y: 2, z: 4, core: 2. Of those that a mesh axis runs over, the one named last changes fastest.
Arguments:
- latents: bfloat16 [1, 2048, 5120], P(None, ('own', 'seq')), may hold values from -6 to 6
- policy_out: bfloat16 [1, 2048, 5120], P(None, ('own', 'seq'), 'tp'), may hold values from -6 to 6
- w_qkv: bfloat16 [16, 5120, 3, 2560], P('own', 'seq', None, 'tp'), may hold values from -0.078125 to 0.078125
- w_out: bfloat16 [16, 2560, 5120], P('own', 'tp', 'seq'), may hold values from -0.125 to 0.125
- qk_gains: bfloat16 [16, 2, 2560], P('own', None, 'tp'), may hold values from 2 to 8
- mod_table: float32 [8, 3, 5120], replicated, may hold values from -3 to 3
- timestep: int32 [1], replicated, may hold values from 0 to 7
- owner: int32 [1], replicated, may hold values from 0 to 15
Outputs:
- block_out: bfloat16 [1, 2048, 5120], P(None, ('own', 'seq'), 'tp')
- sq_err: float32 [1, 2048], P(None, ('own', 'seq'))
The draws below stay inside these ranges and needn't reach their ends.
All inputs are finite; a program needn't handle non-finite values.
Results may differ from the reference program's by a relative error of at most 0.0069.
Values may be sent and summed in bfloat16 or wider, within the bound.
No kernel may reach another device: no remote copies, remote signals or barrier semaphores. Data moves between devices by JAX's collectives and lax.ppermute only.
A program may use at most 192 MiB of HBM per device.

```python
import jax
import jax.numpy as jnp
from jax import lax

D = 5120
HEADS = 20
HD = 128
NSTEP = 8
LAYERS = 1
HW = 2560
SEQ_LEN = 2048
STORED = 16


def draw_qk_gains(key, part):
    key_base = jax.random.fold_in(key, 71)
    base = jax.random.uniform(key_base, (STORED, 2, HW), jnp.float32, 2.0, 2.9)
    gains = base
    return gains.astype(jnp.bfloat16)


def block_levels(key, extent, pieces, smallest, top_value):
    level, own = 1.0, jax.random.fold_in(key, 6)
    for position, blocks in pieces:
        heights = jnp.exp(jax.random.uniform(jax.random.fold_in(own, position), (blocks,), jnp.float32, smallest / len(pieces), top_value / len(pieces)))
        level = level * jnp.repeat(heights, extent[position] // blocks).reshape([-1 if axis == position else 1 for axis in range(len(extent))])
    return level


def noise(rng, shape, width, reach, shards=(), kind=jnp.bfloat16):
    loudness = block_levels(rng, shape, shards, -0.22, 0.18) if shards else 1.0
    values = jax.random.normal(rng, shape, jnp.float32) * width * loudness
    return jnp.minimum(jnp.maximum(values, -reach), reach).astype(kind)


def setup_inputs(seed: int = 0) -> dict:
    key_list = jax.random.split(jax.random.key(seed), 9)
    latents = noise(key_list[0], (1, SEQ_LEN, D), 1.0, 6.0, ((1, 8),))
    policy_out = noise(key_list[1], (1, SEQ_LEN, D), 1.0, 6.0, ((1, 8), (2, 4)))
    w_qkv = noise(key_list[2], (STORED, D, 3, HW), D ** -0.5, 0.078125, ((0, 4), (1, 2), (3, 4)))
    w_out = noise(key_list[3], (STORED, HW, D), HW ** -0.5, 0.125, ((0, 4), (1, 4), (2, 2)))
    qk_gains = draw_qk_gains(jax.random.fold_in(key_list[8], 71), 0)
    mod_table = noise(key_list[5], (NSTEP, 3, D), 0.5, 3.0, (), jnp.float32)
    timestep = jax.random.randint(key_list[6], (1,), 0, NSTEP).astype(jnp.int32)
    owner = jax.random.randint(key_list[7], (LAYERS,), 0, STORED).astype(jnp.int32)
    return dict(latents=latents, policy_out=policy_out, w_qkv=w_qkv, w_out=w_out, qk_gains=qk_gains, mod_table=mod_table, timestep=timestep, owner=owner)


def reference(latents, policy_out, w_qkv, w_out, qk_gains, mod_table, timestep, owner):
    root = owner[0]
    weights_qkv = lax.dynamic_index_in_dim(w_qkv, root, 0, keepdims=False)
    weights_out = lax.dynamic_index_in_dim(w_out, root, 0, keepdims=False)
    gains = lax.dynamic_index_in_dim(qk_gains, root, 0, keepdims=False).astype(jnp.float32)
    onehot = (jnp.arange(NSTEP, dtype=jnp.int32) == timestep[0]).astype(jnp.float32)
    modulation = jnp.tensordot(onehot, mod_table, axes=1, precision=lax.Precision.HIGHEST)
    shift, scale, gate = (modulation[0], modulation[1], modulation[2])
    inputs = latents[0].astype(jnp.float32)
    center = lax.optimization_barrier(jnp.mean(inputs, axis=-1, keepdims=True))
    spread = lax.optimization_barrier(jnp.mean((inputs - center) ** 2, axis=-1, keepdims=True))
    normed = (inputs - center) * lax.rsqrt(spread + 1e-06)
    modulated = (normed * (1.0 + scale) + shift).astype(jnp.bfloat16)
    qkv = jnp.dot(modulated, weights_qkv.reshape(D, 3 * HW), preferred_element_type=jnp.float32)
    qkv = qkv.reshape(SEQ_LEN, 3, HW)
    query, key, value = (qkv[:, 0], qkv[:, 1], qkv[:, 2])
    query = (query * lax.rsqrt(lax.optimization_barrier(jnp.mean(query * query, axis=-1, keepdims=True)) + 1e-06) * gains[0]).astype(jnp.bfloat16)
    key = (key * lax.rsqrt(lax.optimization_barrier(jnp.mean(key * key, axis=-1, keepdims=True)) + 1e-06) * gains[1]).astype(jnp.bfloat16)
    value = value.astype(jnp.bfloat16)
    query = query.reshape(SEQ_LEN, HEADS, HD).transpose(1, 0, 2)
    key = key.reshape(SEQ_LEN, HEADS, HD).transpose(1, 0, 2)
    value = value.reshape(SEQ_LEN, HEADS, HD).transpose(1, 0, 2)

    def one_head(triple):
        head_q, head_k, head_v = triple
        scores = jnp.dot(head_q, head_k.T, preferred_element_type=jnp.float32) * (1.0 / HD ** 0.5)
        probs = jnp.exp(scores - lax.optimization_barrier(jnp.max(scores, axis=-1, keepdims=True)))
        totals = lax.optimization_barrier(jnp.sum(probs, axis=-1, keepdims=True))
        mixed = jnp.dot(probs.astype(jnp.bfloat16), head_v, preferred_element_type=jnp.float32)
        return (mixed / totals).astype(jnp.bfloat16)
    attn = lax.map(one_head, (query, key, value))
    attn = attn.transpose(1, 0, 2).reshape(SEQ_LEN, HW)
    proj = jnp.dot(attn, weights_out, preferred_element_type=jnp.float32)
    block = (inputs + gate * proj).astype(jnp.bfloat16)
    differ = block.astype(jnp.float32) - policy_out[0].astype(jnp.float32)
    squares = lax.optimization_barrier(jnp.mean(differ * differ, axis=-1))
    return (block[None], squares[None])
```

```python
import functools

import jax
import jax.numpy as jnp
from jax import lax
from jax.experimental import pallas as pl
from jax.experimental.pallas import tpu as pltpu
from jax.sharding import PartitionSpec as P

HD = 128
BLOCKS = 4
EPS = 1e-06


def call(kernel, out_shape, **kwargs):
    return pl.pallas_call(
        kernel,
        out_shape=out_shape,
        compiler_params=pltpu.CompilerParams(vmem_limit_bytes=48 * 2**20),
        cost_estimate=pl.CostEstimate(flops=0, bytes_accessed=0, transcendentals=0),
        **kwargs,
    )


def after(value, *first):
    return lax.optimization_barrier((value, *first))[0]


def modulate_kernel(ints_ref, x_ref, table_ref, *refs):
    out_refs, whole = refs[:-1], refs[-1]
    step, start = ints_ref[0], ints_ref[1]
    x = x_ref[...].astype(jnp.float32)
    center = jnp.mean(x, axis=-1, keepdims=True)
    spread = jnp.mean((x - center) ** 2, axis=-1, keepdims=True)
    normed = (x - center) * lax.rsqrt(spread + EPS)
    shift = table_ref[0, pl.ds(step, 1), :]
    scale = table_ref[1, pl.ds(step, 1), :]
    whole[...] = normed * (1.0 + scale) + shift
    pieces, width = len(out_refs), out_refs[0].shape[1]
    for d in range(pieces):
        place = lax.rem(start + d, pieces) * width
        out_refs[d][...] = whole[:, pl.ds(pl.multiple_of(place, width), width)].astype(jnp.bfloat16)


def modulate(x, table, step, start, pieces):
    rows, width = x.shape
    tile = min(rows, 64)
    part = width // pieces
    return call(
        modulate_kernel,
        [jax.ShapeDtypeStruct((rows, part), jnp.bfloat16)] * pieces,
        grid_spec=pltpu.PrefetchScalarGridSpec(
            num_scalar_prefetch=1,
            grid=(rows // tile,),
            in_specs=[
                pl.BlockSpec((tile, width), lambda i, s: (i, 0)),
                pl.BlockSpec((2, *table.shape[1:]), lambda i, s: (0, 0, 0)),
            ],
            out_specs=[pl.BlockSpec((tile, part), lambda i, s: (i, 0))] * pieces,
            scratch_shapes=[pltpu.VMEM((tile, width), jnp.float32)],
        ),
    )(jnp.stack([step, start]), x, table)


def unit_count(full, rest, with_query):
    return 3 * full + 2 * rest + (rest if with_query else 0)


def project_kernel(full, rest, queries, parts, ints_ref, *refs):
    n_blocks, places = len(queries), len(queries[0])
    x_refs, (mine_ref, got_ref) = refs[:n_blocks], refs[n_blocks : n_blocks + 2]
    out_refs, (w, x, sems) = refs[n_blocks + 2 : -3], refs[-3:]
    kinds, depth, _ = got_ref.shape
    rows = x_refs[0].shape[0]
    step = depth // parts

    def copy(source, kind, part):
        some = pl.ds(part * step, step)
        return pltpu.make_async_copy(source.at[kind, some], w.at[kind, some], sems.at[kind, part])

    for used, source in ((1, mine_ref.at[ints_ref[1]]), (0, got_ref)):

        @pl.when(ints_ref[0] == used)
        def _(source=source):
            for kind in range(kinds):
                for part in range(parts):
                    copy(source, kind, part).start()

    for b in range(n_blocks):
        x[b * rows : (b + 1) * rows, :] = x_refs[b][...]
    firsts = [full * lax.rem(ints_ref[2] + d, places) for d in range(places)]
    for kind in range(kinds):
        for part in range(parts):
            copy(got_ref, kind, part).wait()
        res = jnp.dot(x[...], w[kind], preferred_element_type=jnp.float32)
        heads = [res[:, i * HD : (i + 1) * HD] for i in range(res.shape[1] // HD)]
        for d, out_ref in enumerate(out_refs):
            base = 0
            for b in range(n_blocks):
                some = slice(b * rows, (b + 1) * rows)
                for i in range(full):
                    value = heads[i][some]
                    for place in range(1, places):
                        value = jnp.where(firsts[d] == full * place, heads[full * place + i][some], value)
                    out_ref[base + kind * full + i] = value.astype(out_ref.dtype)
                for i in range(rest):
                    value = heads[full * places + i][some].astype(out_ref.dtype)
                    if kind:
                        out_ref[base + 3 * full + (kind - 1) * rest + i] = value
                    elif queries[b][d]:
                        out_ref[base + 3 * full + 2 * rest + i] = value
                base += unit_count(full, rest, queries[b][d])


def project(blocks, mine, got, ints, full, rest, queries):
    rows, depth = blocks[0].shape
    kinds, _, cols = got.shape
    places = len(queries[0])
    shapes = [(sum(unit_count(full, rest, q[d]) for q in queries), rows, HD) for d in range(places)]
    types = [jnp.float32] + [jnp.bfloat16] * (places - 1)
    parts = 2 if depth % 32 == 0 else 1
    return call(
        functools.partial(project_kernel, full, rest, queries, parts),
        [jax.ShapeDtypeStruct(s, t) for s, t in zip(shapes, types)],
        grid_spec=pltpu.PrefetchScalarGridSpec(
            num_scalar_prefetch=1,
            grid=(1,),
            in_specs=[pl.BlockSpec((rows, depth), lambda i, s: (0, 0))] * len(blocks)
            + [pl.BlockSpec(memory_space=pl.ANY)] * 2,
            out_specs=[pl.BlockSpec(s, lambda i, s: (0, 0, 0)) for s in shapes],
            scratch_shapes=[
                pltpu.VMEM((kinds, depth, cols), jnp.bfloat16),
                pltpu.VMEM((len(blocks) * rows, depth), jnp.bfloat16),
                pltpu.SemaphoreType.DMA((kinds, parts)),
            ],
        ),
    )(ints, *blocks, mine, got)


def combine_kernel(full, rest, homes, own_at, got_at, n_arrays, *refs):
    arrays, gains_ref, out_refs = refs[:n_arrays], refs[n_arrays], refs[n_arrays + 1 :]
    q_refs, (kv_ref, sq_ref) = out_refs[:-2], out_refs[-2:]
    heads = full + rest
    rows = kv_ref.shape[1]
    ones = jnp.ones((8, HD), jnp.float32)
    q_refs = list(q_refs)
    for place, home in enumerate(homes):
        sources = [own_at[place], *got_at[place]]

        def total(unit):
            out = None
            for array, base in sources:
                value = arrays[array][base + unit].astype(jnp.float32)
                out = value if out is None else out + value
            return out

        n_q = full + (rest if home else 0)
        q_ref = q_refs.pop(0) if n_q else None
        squares = [jnp.zeros((rows, HD), jnp.float32)] * 2
        for i in range(n_q):
            query = total(i if i < full else 3 * full + 2 * rest + i - full)
            squares[0] = squares[0] + query * query
            q_ref[i] = (query * gains_ref[0, i : i + 1, :]).astype(jnp.bfloat16)
        first = place * 2 * heads
        for i in range(heads):
            key = total(full + i if i < full else 3 * full + i - full)
            if i < full or home:
                squares[1] = squares[1] + key * key
            kv_ref[first + i] = (key * gains_ref[1, i : i + 1, :]).astype(jnp.bfloat16)
            value = total(2 * full + i if i < full else 3 * full + rest + i - full)
            kv_ref[first + heads + i] = value.astype(jnp.bfloat16)
        for which in range(2):
            sums = lax.dot_general(
                ones,
                squares[which],
                (((1,), (1,)), ((), ())),
                precision=lax.Precision.HIGHEST,
                preferred_element_type=jnp.float32,
            )
            sq_ref[which, place : place + 1, :] = sums[:1]


def combine(own, got, gains, full, rest, homes):
    arrays = []
    for value, _ in own + [pair for pairs in got for pair in pairs]:
        if not any(value is other for other in arrays):
            arrays.append(value)

    def place(pair):
        return [i for i, value in enumerate(arrays) if value is pair[0]][0], pair[1]

    rows = arrays[0].shape[1]
    counts = [full + (rest if home else 0) for home in homes]
    shapes = [(n, rows, HD) for n in counts if n]
    shapes += [(len(homes) * 2 * (full + rest), rows, HD), (2, len(homes), rows)]
    types = [jnp.bfloat16] * (len(shapes) - 1) + [jnp.float32]
    out = call(
        functools.partial(
            combine_kernel,
            full,
            rest,
            homes,
            [place(pair) for pair in own],
            [[place(pair) for pair in pairs] for pairs in got],
            len(arrays),
        ),
        [jax.ShapeDtypeStruct(s, t) for s, t in zip(shapes, types)],
    )(*arrays, gains)
    queries = list(out[:-2])
    return [queries.pop(0) if n else None for n in counts], out[-2], out[-1]


def attend_kernel(block, places, total_width, q_ref, *refs):
    out_ref = refs[-1]
    n_kv = places[0] * places[1]
    k_refs, v_refs, sum_refs = refs[:n_kv], refs[n_kv : 2 * n_kv], refs[2 * n_kv : -1]
    rows = q_ref.shape[1]
    scale = 1.4426950408889634 / HD**0.5
    query = q_ref[0]
    norm = lax.rsqrt(sum_refs[0][0, block : block + 1, :] / total_width + EPS) * scale
    norm = jnp.broadcast_to(norm, (8, rows)).T[:, :1]
    scores, peak = [], None
    for j in range(n_kv):
        sums = sum_refs[j // places[1]][1, j % places[1] : j % places[1] + 1, :]
        s = lax.dot_general(query, k_refs[j][0], (((1,), (1,)), ((), ())), preferred_element_type=jnp.float32)
        s = s * lax.rsqrt(sums / total_width + EPS)
        scores.append(s)
        top = jnp.max(s, axis=-1, keepdims=True)
        peak = top if peak is None else jnp.maximum(peak, top)
    mixed, weight = None, None
    for j in range(n_kv):
        probs = jnp.exp2((scores[j] - peak) * norm)
        part = jnp.sum(probs, axis=-1, keepdims=True)
        out = jnp.dot(probs.astype(jnp.bfloat16), v_refs[j][0], preferred_element_type=jnp.float32)
        mixed = out if mixed is None else mixed + out
        weight = part if weight is None else weight + part
    out_ref[0] = (mixed / weight).astype(out_ref.dtype)


def attend(block, queries, kv, sums, total_width, heads):
    units, rows, _ = queries.shape
    one = (1, rows, HD)
    flat = [(array, d) for core in kv for array in core for d in range(array.shape[0] // (2 * heads))]
    shape = (len(kv), len(flat) // len(kv))

    def spec(first):
        return pl.BlockSpec(one, lambda u: (first + u, 0, 0))

    return call(
        functools.partial(attend_kernel, block, shape, total_width),
        jax.ShapeDtypeStruct((units, rows, HD), jnp.bfloat16),
        grid=(units,),
        in_specs=[spec(0)]
        + [spec(d * 2 * heads) for _, d in flat]
        + [spec(d * 2 * heads + heads) for _, d in flat]
        + [pl.BlockSpec(s.shape, lambda u: (0, 0, 0)) for s in sums],
        out_specs=spec(0),
    )(queries, *[a for a, _ in flat], *[a for a, _ in flat], *sums)


def output_kernel(parts, ints_ref, own_ref, other_ref, *refs):
    w_refs, (out_ref, joined, w, sems) = refs[:-4], refs[-4:]
    heads = own_ref.shape[0]
    step = w.shape[1] // parts

    cores = len(w_refs) // 2
    half = w.shape[2]

    def copy(source, which, part):
        some = pl.ds(part * step, step)
        return pltpu.make_async_copy(source.at[some], w.at[which, some], sems.at[which, part])

    for i in range(2):

        @pl.when(ints_ref[0] == i)
        def _(i=i):
            for part in range(parts):
                for which in range(cores):
                    copy(w_refs[i * cores + which], which, part).start()

    for part, ref in enumerate((own_ref, other_ref)):
        for i in range(heads):
            joined[:, (part * heads + i) * HD : (part * heads + i + 1) * HD] = ref[i]
    totals = [None] * cores
    for part in range(parts):
        some = slice(part * step, (part + 1) * step)
        for which in range(cores):
            copy(w_refs[0], which, part).wait()
            out = jnp.dot(joined[:, some], w[which, some, :], preferred_element_type=jnp.float32)
            totals[which] = out if part == 0 else totals[which] + out
    for which in range(cores):
        first = lax.rem(ints_ref[1] + which, cores) * half
        out_ref[:, pl.ds(pl.multiple_of(first, half), half)] = totals[which].astype(out_ref.dtype)


def output(which, own, other, weights, kind):
    heads, rows, _ = own.shape
    depth, half = weights[0].shape
    cores = len(weights) // 2
    cols = half * cores
    parts = 2
    return call(
        functools.partial(output_kernel, parts),
        jax.ShapeDtypeStruct((rows, cols), kind),
        grid_spec=pltpu.PrefetchScalarGridSpec(
            num_scalar_prefetch=1,
            grid=(1,),
            in_specs=[pl.BlockSpec(own.shape, lambda j, s: (0, 0, 0))] * 2
            + [pl.BlockSpec(memory_space=pl.ANY)] * len(weights),
            out_specs=pl.BlockSpec((rows, cols), lambda j, s: (0, 0)),
            scratch_shapes=[
                pltpu.VMEM((rows, depth), jnp.bfloat16),
                pltpu.VMEM((cores, depth, half), jnp.bfloat16),
                pltpu.SemaphoreType.DMA((cores, parts)),
            ],
        ),
    )(which, own, other, *weights)


def pair_of(n_own, n_seq):
    fits = [p for p in range(1, n_own) if n_own % p == 0 and n_own // p * n_seq <= BLOCKS]
    return fits[0] if fits else n_own


def run(sizes, root_g, latents, policy_out, w_qkv, w_out, qk_gains, mod_table, timestep, owner):
    n_own, n_seq, n_tp = sizes
    pair = pair_of(n_own, n_seq)
    groups = n_own // pair
    root = owner[0] // w_qkv.shape[0]
    root_c = root % pair
    own, y, z = lax.axis_index("own"), lax.axis_index("seq"), lax.axis_index("tp")
    group, core = own // pair, own % pair
    both = ("own", "seq")

    def at(g, c, s):
        return ((g + root_g) % groups * pair + c) * n_seq + s % n_seq

    def send(value, a, b, d):
        return lax.ppermute(value, both, [(at(a, c, s), at(b, c, s + d)) for c in range(pair) for s in range(n_seq)])

    def shift(value, dc, d=0):
        perm = [(at(g, c, s), at(g, (c + dc) % pair, s + d)) for g in range(groups) for c in range(pair) for s in range(n_seq)]
        return lax.ppermute(value, both, perm)

    def of_root_core(value):
        out = value
        for dc in range(1, pair):
            got = shift(value, dc)
            out = got if pair == 2 else jnp.where((core - dc) % pair == root_c, got, out)
        return out

    stored = owner[0] % w_qkv.shape[0]
    rows, width = latents.shape[1:]
    cols = w_qkv.shape[3]
    heads = cols // HD
    full, rest = heads // n_seq, heads % n_seq
    share_cols = width // n_tp

    pieces = modulate(latents[0], mod_table.transpose(1, 0, 2), timestep[0], y, n_seq)
    blocks = {(0, 0): pieces[0]}
    for dg in range(1, groups):
        blocks[dg, 0] = send(pieces[0], dg, 0, 0)
    for d in range(1, n_seq):
        blocks[0, d] = lax.ppermute(pieces[d], "seq", [(s, (s + d) % n_seq) for s in range(n_seq)])

    kinds_first = w_qkv.transpose(0, 2, 1, 3)
    stored_now = stored
    mine = lax.dynamic_index_in_dim(kinds_first, stored_now, 0, keepdims=False)
    mine_gains = lax.dynamic_index_in_dim(qk_gains, stored_now, 0, keepdims=False)

    got_weights = of_root_core(mine)
    gains = jnp.where(core == root_c, mine_gains, of_root_core(mine_gains))
    gains = gains.astype(jnp.float32).reshape(2, heads, HD)
    gains = jnp.concatenate([lax.dynamic_slice_in_dim(gains, full * y, full, 1), gains[:, full * n_seq :]], 1)
    ints = jnp.stack([(own == root).astype(jnp.int32), stored, y])

    paired = n_tp == 2 * n_seq and n_seq == 2 and groups > 1 and pair == 2 and share_cols % (pair * HD) == 0
    if paired:
        half = share_cols // pair
        stored_now = after(stored, mine)
        quarters = lax.dynamic_index_in_dim(w_out, stored_now, 0, keepdims=False)

        def of_quarter(quarter, part):
            return lax.dynamic_slice_in_dim(quarters, quarter * share_cols + part * half, half, 1)

        keep, give = z % 2, 1 - z % 2
        got = shift(jnp.stack([of_quarter(keep, 1 - core), of_quarter(give, 1 - core)]), 1)
        here = jnp.stack([of_quarter(keep, core), of_quarter(give, core)])
        here = jnp.where(core == root_c, here, got)
        keep, give = here[0], here[1]
        taken = lax.ppermute(give, "tp", [(t, t ^ 1) for t in range(n_tp)])
        near = [keep, taken]
        far_near = [[send(keep, 0, dg, 0)] for dg in range(1, groups)]
    for dg in range(1, groups):
        for d in range(1, n_seq):
            blocks[dg, d] = send(blocks[0, d], dg, 0, 0)

    early = [key for key in sorted(blocks) if key[0] == 0 or key[1] == 0]
    late = [key for key in sorted(blocks) if key not in early]
    chunks = [[(0, 0)]] + [part[i : i + 2] for part in (early[1:], late) for i in range(0, len(part), 2)]
    own_part, other_part, arrivals = {}, {}, []
    previous, hops = None, []
    for number, chunk in enumerate(chunks):
        queries = [[(d + dd) % n_seq == 0 for dd in range(n_seq)] for _, d in chunk]
        x = [blocks[key] for key in chunk]
        if previous is not None:
            x[0] = after(x[0], previous, *arrivals[: number - 1])
        if number == 0:
            x[0] = after(x[0], gains, *[blocks[key] for key in early[1:]])
        parts = project(x, kinds_first, got_weights, ints, full, rest, queries)
        previous = parts[0]
        base = 0
        for key, q in zip(chunk, queries):
            own_part[key] = (parts[0], base)
            base += unit_count(full, rest, q[0])
        for dd in range(1, n_seq):
            got = send(parts[dd], 0, 0, dd)
            arrivals.append(got)
            base = 0
            for (dg, d), q in zip(chunk, queries):
                other_part.setdefault((dg, (d + dd) % n_seq), []).append((got, base))
                base += unit_count(full, rest, q[dd])
        if paired and number == 0:
            for dg in range(1, groups):
                far_near[dg - 1].append(send(after(near[1], previous), 0, dg, 0))
    last = previous

    def chosen(here, there, first):
        out = jnp.concatenate([after(value, first) for value in here], 0)
        for dg in range(1, groups):
            values = jnp.concatenate([after(value, first) for value in there[dg - 1]], 0)
            out = jnp.where(group == (root_g + dg) % groups, values, out)
        return [out, shift(out, 1)]

    if paired:
        far_far = [[send(after(values[0], arrivals[0]), dg + 1, dg + 1, 1)] for dg, values in enumerate(far_near)]
        for dg, values in enumerate(far_near):
            far_far[dg].append(send(after(values[1], last), dg + 1, dg + 1, 1))
        back = [send(after(far_far[0][0], last), 1, 0, 0)]
        near_w = chosen(near, far_near, last)
    combined = []
    order = sorted(blocks)
    for keys in [order[i : i + 2] for i in range(0, len(order), 2)]:
        combined.append(
            combine(
                [own_part[key] for key in keys],
                [other_part.get(key, []) for key in keys],
                after(gains, last),
                full,
                rest,
                [d == 0 for _, d in keys],
            )
        )
    last = combined[-1][2]
    if paired:
        back.append(send(after(far_far[0][1], last), 1, 0, 0))

    sums = jnp.concatenate([part[2] for part in combined], 1)
    parts = [sums]
    for d in range(1, n_tp):
        parts.append(lax.ppermute(sums, "tp", [(t, (t + d) % n_tp) for t in range(n_tp)]))
    sums = sum(parts[1:], parts[0])

    def moved(value, d):
        value = value.reshape(2, groups, n_seq, rows)
        return jnp.concatenate([value[:, :, n_seq - d :], value[:, :, : n_seq - d]], 2).reshape(2, groups * n_seq, rows)

    all_sums, all_kv = [], []
    kv = [part[1] for part in combined]
    for dc in range(pair):
        here = None
        for d in range(n_seq):
            got = sums
            if dc or d:
                got = shift(sums, dc, d)
            got = moved(got, d) if d else got
            here = got if here is None else here + got
        all_sums.append(here)
        if dc:
            all_kv.append([shift(value, dc) for value in kv])
        else:
            all_kv.append(kv)

    arrived = {}
    for key in sorted(order, key=lambda key: (-key[0], -key[1])):
        query = combined[order.index(key) // 2][0][order.index(key) % 2]
        if query is None:
            continue
        if arrived:
            query = after(query, previous)
        result = attend(order.index(key), query, all_kv, all_sums, cols * n_tp, full + rest)
        previous = result
        dg, d = key
        arrived[key] = send(result, 0, dg, -d) if key != (0, 0) else result
    from_seq = []
    at_rest = None
    for d in range(n_seq):
        if (0, d) not in arrived:
            continue
        here = arrived[0, d]
        for dg in range(1, groups):
            here = jnp.where(group == (root_g + dg) % groups, arrived[dg, d], here)
        from_seq.append(here[:full])
        if d == 0:
            at_rest = here[full:]
    turn = (jnp.arange(n_seq) - y) % n_seq
    if full:
        if n_seq == 2:
            ordered = jnp.concatenate(
                [jnp.where(y == 0, from_seq[0], from_seq[1]), jnp.where(y == 0, from_seq[1], from_seq[0]), at_rest], 0
            )
        else:
            ordered = jnp.take(jnp.stack(from_seq), turn, axis=0).reshape(n_seq * full, rows, HD)
            ordered = jnp.concatenate([ordered, at_rest], 0)
    else:
        ordered = at_rest

    if paired:
        out_weights = near_w + chosen(back, far_far, all_sums[0])
        other = lax.ppermute(ordered, "tp", [(t, t ^ 1) for t in range(n_tp)])
        mine_first = (y == z // 2).astype(jnp.int32)
        sent = output(jnp.stack([mine_first, core]), ordered, other, out_weights, jnp.bfloat16)
        got = lax.ppermute(sent, "tp", [(t, (t + 2) % n_tp) for t in range(n_tp)])
        kept = output(jnp.stack([1 - mine_first, core]), ordered, after(other, sent), out_weights, jnp.float32)
        share = kept + got.astype(jnp.float32)
    else:
        attn = ordered.transpose(1, 0, 2).reshape(rows, cols)
        mine_out = lax.dynamic_index_in_dim(w_out, stored, 0, keepdims=False)
        spread_out = mine_out
        for dg in range(1, groups):
            got = send(mine_out, 0, dg, 0)
            spread_out = jnp.where(group == (root_g + dg) % groups, got, spread_out)
        parts = [spread_out]
        for d in range(1, n_seq):
            parts.append(shift(spread_out, 0, d))
        out_w = jnp.take(jnp.stack(parts), (y - jnp.arange(n_seq)) % n_seq, axis=0)
        out_w = jnp.where(core == root_c, out_w, of_root_core(out_w))
        proj = jnp.einsum("tk,skn->tsn", attn, out_w, preferred_element_type=jnp.float32)
        proj = proj.reshape(rows, n_tp, share_cols).transpose(1, 0, 2)
        sent = proj.astype(jnp.bfloat16)
        share = lax.dynamic_index_in_dim(proj, z, 0, keepdims=False)
        for d in range(1, n_tp):
            piece = lax.dynamic_index_in_dim(sent, (z + d) % n_tp, 0, keepdims=False)
            got = lax.ppermute(piece, "tp", [(t, (t + d) % n_tp) for t in range(n_tp)])
            share = share + got.astype(jnp.float32)
    inputs = lax.dynamic_slice_in_dim(latents[0], z * share_cols, share_cols, 1).astype(jnp.float32)
    gate = lax.dynamic_slice(mod_table, (timestep[0], 2, z * share_cols), (1, 1, share_cols))[0]
    block = (inputs + gate * share).astype(jnp.bfloat16)
    differ = block.astype(jnp.float32) - policy_out[0].astype(jnp.float32)
    squares = lax.psum(jnp.sum(differ * differ, axis=-1), "tp") / width
    return lax.optimization_barrier((block[None], squares[None]))


def local(sizes, *args):
    w_qkv, owner = args[2], args[7]
    pair = pair_of(*sizes[:2])
    branches = [functools.partial(run, sizes, g) for g in range(sizes[0] // pair)]
    return lax.switch(owner[0] // w_qkv.shape[0] // pair, branches, *args)


def solution(mesh):
    placed = (
        P(None, ("own", "seq"), None),
        P(None, ("own", "seq"), "tp"),
        P("own", "seq", None, "tp"),
        P("own", "tp", "seq"),
        P("own", None, "tp"),
        P(),
        P(),
        P(),
    )
    sizes = tuple(mesh.shape[axis] for axis in ("own", "seq", "tp"))
    return jax.shard_map(
        functools.partial(local, sizes),
        mesh=mesh,
        in_specs=placed,
        out_specs=(P(None, ("own", "seq"), "tp"), P(None, ("own", "seq"))),
        check_vma=False,
    )
```

```python
import functools

import jax
import jax.numpy as jnp
from jax import lax
from jax.experimental import pallas as pl
from jax.experimental.pallas import tpu as pltpu
from jax.sharding import PartitionSpec as P

HD = 128
BLOCKS = 4
EPS = 1e-06


def call(kernel, out_shape, flops=0, mib=24, **kwargs):
    return pl.pallas_call(
        kernel,
        out_shape=out_shape,
        compiler_params=pltpu.CompilerParams(vmem_limit_bytes=mib * 2**20),
        cost_estimate=pl.CostEstimate(flops=flops, bytes_accessed=0, transcendentals=0),
        **kwargs,
    )


def after(value, *first):
    return lax.optimization_barrier((value, *first))[0]


def prepare_kernel(pieces, n_cols, ints_ref, x_ref, table_ref, w_ref, w_out_ref, *refs):
    out_refs, (w_copy, out_copy, whole, w_held, out_held, sems) = refs[:pieces], refs[pieces:]
    step, start, stored = ints_ref[0], ints_ref[1], ints_ref[2]
    kinds, width = w_held.shape[0], out_held.shape[2]
    ways = [(w_ref.at[stored, i], w_held.at[i], w_copy.at[i]) for i in range(kinds)]
    for i in range(n_cols):
        some = pl.ds(pl.multiple_of(ints_ref[3 + i], HD), width)
        ways.append((w_out_ref.at[stored, :, some], out_held.at[i], out_copy.at[i]))
    into = [pltpu.make_async_copy(a, b, sems.at[0, i]) for i, (a, b, _) in enumerate(ways)]
    onward = [pltpu.make_async_copy(b, c, sems.at[1, i]) for i, (_, b, c) in enumerate(ways)]
    turn, turns = pl.program_id(0), pl.num_programs(0)

    @pl.when(turn == 0)
    def _():
        for copy in into:
            copy.start()

    for i in range(len(ways)):

        @pl.when(turn == jnp.minimum(1 + i, turns - 1))
        def _(i=i):
            into[i].wait()
            onward[i].start()

    x = x_ref[...].astype(jnp.float32)
    center = jnp.mean(x, axis=-1, keepdims=True)
    spread = jnp.mean((x - center) ** 2, axis=-1, keepdims=True)
    normed = (x - center) * lax.rsqrt(spread + EPS)
    shift = table_ref[0, pl.ds(step, 1), :]
    scale = table_ref[1, pl.ds(step, 1), :]
    whole[...] = normed * (1.0 + scale) + shift
    width = out_refs[0].shape[1]
    for d in range(pieces):
        place = lax.rem(start + d, pieces) * width
        out_refs[d][...] = whole[:, pl.ds(pl.multiple_of(place, width), width)].astype(jnp.bfloat16)

    @pl.when(turn == turns - 1)
    def _():
        for copy in onward:
            copy.wait()


def prepare(x, table, w, w_out, ints, pieces, width_out):
    rows, width = x.shape
    tile = min(rows, 64)
    part = width // pieces
    n_cols = ints.shape[0] - 3
    any_space = pl.BlockSpec(memory_space=pl.ANY)
    out = call(
        functools.partial(prepare_kernel, pieces, n_cols),
        [jax.ShapeDtypeStruct((rows, part), jnp.bfloat16)] * pieces
        + [
            jax.ShapeDtypeStruct(w.shape[1:], w.dtype),
            jax.ShapeDtypeStruct((max(n_cols, 1), w_out.shape[1], width_out), w_out.dtype),
        ],
        mib=40,
        grid_spec=pltpu.PrefetchScalarGridSpec(
            num_scalar_prefetch=1,
            grid=(rows // tile,),
            in_specs=[
                pl.BlockSpec((tile, width), lambda i, s: (i, 0)),
                pl.BlockSpec((2, *table.shape[1:]), lambda i, s: (0, 0, 0)),
                any_space,
                any_space,
            ],
            out_specs=[pl.BlockSpec((tile, part), lambda i, s: (i, 0))] * pieces + [any_space] * 2,
            scratch_shapes=[
                pltpu.VMEM((tile, width), jnp.float32),
                pltpu.VMEM(w.shape[1:], w.dtype),
                pltpu.VMEM((max(n_cols, 1), w_out.shape[1], width_out), w_out.dtype),
                pltpu.SemaphoreType.DMA((2, w.shape[1] + max(n_cols, 1))),
            ],
        ),
    )(ints, x, table, w, w_out)
    return out[:pieces], out[-2], out[-1]


def unit_count(full, rest, with_query):
    return 3 * full + 2 * rest + (rest if with_query else 0)


def project_kernel(full, rest, queries, parts, ints_ref, *refs):
    n_blocks, places = len(queries), len(queries[0])
    x_refs, (mine_ref, got_ref) = refs[:n_blocks], refs[n_blocks : n_blocks + 2]
    out_refs, (w, x, sems) = refs[n_blocks + 2 : -3], refs[-3:]
    kinds, depth, _ = got_ref.shape
    rows = x_refs[0].shape[0]
    step = depth // parts

    def copy(source, kind, part):
        some = pl.ds(part * step, step)
        return pltpu.make_async_copy(source.at[kind, some], w.at[kind, some], sems.at[kind, part])

    for used, source in ((1, mine_ref.at[ints_ref[1]]), (0, got_ref)):

        @pl.when(ints_ref[0] == used)
        def _(source=source):
            for kind in range(kinds):
                for part in range(parts):
                    copy(source, kind, part).start()

    for b in range(n_blocks):
        x[b * rows : (b + 1) * rows, :] = x_refs[b][...]
    firsts = [full * lax.rem(ints_ref[2] + d, places) for d in range(places)]
    for kind in range(kinds):
        for part in range(parts):
            copy(got_ref, kind, part).wait()
        res = jnp.dot(x[...], w[kind], preferred_element_type=jnp.float32)
        heads = [res[:, i * HD : (i + 1) * HD] for i in range(res.shape[1] // HD)]
        for d, out_ref in enumerate(out_refs):
            base = 0
            for b in range(n_blocks):
                some = slice(b * rows, (b + 1) * rows)
                for i in range(full):
                    value = heads[i][some]
                    for place in range(1, places):
                        value = jnp.where(firsts[d] == full * place, heads[full * place + i][some], value)
                    out_ref[base + kind * full + i] = value.astype(out_ref.dtype)
                for i in range(rest):
                    value = heads[full * places + i][some].astype(out_ref.dtype)
                    if kind:
                        out_ref[base + 3 * full + (kind - 1) * rest + i] = value
                    elif queries[b][d]:
                        out_ref[base + 3 * full + 2 * rest + i] = value
                base += unit_count(full, rest, queries[b][d])


def project(blocks, mine, got, ints, full, rest, queries):
    rows, depth = blocks[0].shape
    kinds, _, cols = got.shape
    places = len(queries[0])
    shapes = [(sum(unit_count(full, rest, q[d]) for q in queries), rows, HD) for d in range(places)]
    types = [jnp.float32] + [jnp.bfloat16] * (places - 1)
    parts = 2 if depth % 32 == 0 else 1
    return call(
        functools.partial(project_kernel, full, rest, queries, parts),
        [jax.ShapeDtypeStruct(s, t) for s, t in zip(shapes, types)],
        mib=40,
        grid_spec=pltpu.PrefetchScalarGridSpec(
            num_scalar_prefetch=1,
            grid=(1,),
            in_specs=[pl.BlockSpec((rows, depth), lambda i, s: (0, 0))] * len(blocks)
            + [pl.BlockSpec(memory_space=pl.ANY)] * 2,
            out_specs=[pl.BlockSpec(s, lambda i, s: (0, 0, 0)) for s in shapes],
            scratch_shapes=[
                pltpu.VMEM((kinds, depth, cols), jnp.bfloat16),
                pltpu.VMEM((len(blocks) * rows, depth), jnp.bfloat16),
                pltpu.SemaphoreType.DMA((kinds, parts)),
            ],
        ),
    )(ints, *blocks, mine, got)


def combine_kernel(full, rest, homes, own_at, got_at, n_arrays, *refs):
    arrays, gains_ref, out_refs = refs[:n_arrays], refs[n_arrays], refs[n_arrays + 1 :]
    q_refs, (kv_ref, sq_ref) = out_refs[:-2], out_refs[-2:]
    heads = full + rest
    rows = kv_ref.shape[1]
    ones = jnp.ones((8, HD), jnp.float32)
    q_refs = list(q_refs)
    for place, home in enumerate(homes):
        sources = [own_at[place], *got_at[place]]

        def total(unit):
            out = None
            for array, base in sources:
                value = arrays[array][base + unit].astype(jnp.float32)
                out = value if out is None else out + value
            return out

        n_q = full + (rest if home else 0)
        q_ref = q_refs.pop(0) if n_q else None
        squares = [jnp.zeros((rows, HD), jnp.float32)] * 2
        for i in range(n_q):
            query = total(i if i < full else 3 * full + 2 * rest + i - full)
            squares[0] = squares[0] + query * query
            q_ref[i] = (query * gains_ref[0, i : i + 1, :]).astype(jnp.bfloat16)
        first = place * 2 * heads
        for i in range(heads):
            key = total(full + i if i < full else 3 * full + i - full)
            if i < full or home:
                squares[1] = squares[1] + key * key
            kv_ref[first + i] = (key * gains_ref[1, i : i + 1, :]).astype(jnp.bfloat16)
            value = total(2 * full + i if i < full else 3 * full + rest + i - full)
            kv_ref[first + heads + i] = value.astype(jnp.bfloat16)
        for which in range(2):
            sums = lax.dot_general(
                ones,
                squares[which],
                (((1,), (1,)), ((), ())),
                precision=lax.Precision.HIGHEST,
                preferred_element_type=jnp.float32,
            )
            sq_ref[which, place : place + 1, :] = sums[:1]


def combine(own, got, gains, full, rest, homes):
    arrays = []
    for value, _ in own + [pair for pairs in got for pair in pairs]:
        if not any(value is other for other in arrays):
            arrays.append(value)

    def place(pair):
        return [i for i, value in enumerate(arrays) if value is pair[0]][0], pair[1]

    rows = arrays[0].shape[1]
    counts = [full + (rest if home else 0) for home in homes]
    shapes = [(n, rows, HD) for n in counts if n]
    shapes += [(len(homes) * 2 * (full + rest), rows, HD), (2, len(homes), rows)]
    types = [jnp.bfloat16] * (len(shapes) - 1) + [jnp.float32]
    out = call(
        functools.partial(
            combine_kernel,
            full,
            rest,
            homes,
            [place(pair) for pair in own],
            [[place(pair) for pair in pairs] for pairs in got],
            len(arrays),
        ),
        [jax.ShapeDtypeStruct(s, t) for s, t in zip(shapes, types)],
        mib=40,
    )(*arrays, gains)
    queries = list(out[:-2])
    return [queries.pop(0) if n else None for n in counts], out[-2], out[-1]


def attend_kernel(block, n_kv, shape, total_width, q_ref, *refs):
    out_ref = refs[-1]
    k_refs, v_refs, sum_refs = refs[:n_kv], refs[n_kv : 2 * n_kv], refs[2 * n_kv : -1]
    rows = q_ref.shape[1]
    scale = 1.4426950408889634 / HD**0.5
    query = q_ref[0]
    n_blocks, places = shape

    def total(core, which, block):
        out = None
        for d in range(places):
            at = block - block % places + (block - d) % places
            part = sum_refs[core * places + d][which, at : at + 1, :]
            out = part if out is None else out + part
        return out

    norm = lax.rsqrt(total(0, 0, block) / total_width + EPS) * scale
    norm = jnp.broadcast_to(norm, (8, rows)).T[:, :1]
    scores, peak = [], None
    for j in range(n_kv):
        sums = total(j // n_blocks, 1, j % n_blocks)
        s = lax.dot_general(query, k_refs[j][0], (((1,), (1,)), ((), ())), preferred_element_type=jnp.float32)
        s = s * lax.rsqrt(sums / total_width + EPS)
        scores.append(s)
        top = jnp.max(s, axis=-1, keepdims=True)
        peak = top if peak is None else jnp.maximum(peak, top)
    mixed, weight = None, None
    for j in range(n_kv):
        probs = jnp.exp2((scores[j] - peak) * norm)
        part = jnp.sum(probs, axis=-1, keepdims=True)
        out = jnp.dot(probs.astype(jnp.bfloat16), v_refs[j][0], preferred_element_type=jnp.float32)
        mixed = out if mixed is None else mixed + out
        weight = part if weight is None else weight + part
    out_ref[0] = (mixed / weight).astype(out_ref.dtype)


def attend(block, queries, kv, sums, total_width, heads):
    units, rows, _ = queries.shape
    one = (1, rows, HD)
    flat = [(array, d) for core in kv for array in core for d in range(array.shape[0] // (2 * heads))]
    shape = (len(flat) // len(kv), len(sums[0]))
    sums = [array for core in sums for array in core]

    def spec(first):
        return pl.BlockSpec(one, lambda u: (first + u, 0, 0))

    return call(
        functools.partial(attend_kernel, block, len(flat), shape, total_width),
        jax.ShapeDtypeStruct((units, rows, HD), jnp.bfloat16),
        grid=(units,),
        in_specs=[spec(0)]
        + [spec(d * 2 * heads) for _, d in flat]
        + [spec(d * 2 * heads + heads) for _, d in flat]
        + [pl.BlockSpec(s.shape, lambda u: (0, 0, 0)) for s in sums],
        out_specs=spec(0),
    )(queries, *[a for a, _ in flat], *[a for a, _ in flat], *sums)


def output_kernel(parts, ints_ref, own_ref, other_ref, *refs):
    w_refs, (out_ref, joined, w, sems) = refs[:-4], refs[-4:]
    heads = own_ref.shape[0]
    step = w.shape[1] // parts

    cores = len(w_refs) // 2
    half = w.shape[2]

    def copy(source, which, part):
        some = pl.ds(part * step, step)
        return pltpu.make_async_copy(source.at[some], w.at[which, some], sems.at[which, part])

    for i in range(2):

        @pl.when(ints_ref[0] == i)
        def _(i=i):
            for part in range(parts):
                for which in range(cores):
                    copy(w_refs[i * cores + which], which, part).start()

    for part, ref in enumerate((own_ref, other_ref)):
        for i in range(heads):
            joined[:, (part * heads + i) * HD : (part * heads + i + 1) * HD] = ref[i]
    totals = [None] * cores
    for part in range(parts):
        some = slice(part * step, (part + 1) * step)
        for which in range(cores):
            copy(w_refs[0], which, part).wait()
            out = jnp.dot(joined[:, some], w[which, some, :], preferred_element_type=jnp.float32)
            totals[which] = out if part == 0 else totals[which] + out
    for which in range(cores):
        first = lax.rem(ints_ref[1] + which, cores) * half
        out_ref[:, pl.ds(pl.multiple_of(first, half), half)] = totals[which].astype(out_ref.dtype)


def output(which, own, other, weights, kind):
    heads, rows, _ = own.shape
    depth, half = weights[0].shape
    cores = len(weights) // 2
    cols = half * cores
    parts = 2
    return call(
        functools.partial(output_kernel, parts),
        jax.ShapeDtypeStruct((rows, cols), kind),
        grid_spec=pltpu.PrefetchScalarGridSpec(
            num_scalar_prefetch=1,
            grid=(1,),
            in_specs=[pl.BlockSpec(own.shape, lambda j, s: (0, 0, 0))] * 2
            + [pl.BlockSpec(memory_space=pl.ANY)] * len(weights),
            out_specs=pl.BlockSpec((rows, cols), lambda j, s: (0, 0)),
            scratch_shapes=[
                pltpu.VMEM((rows, depth), jnp.bfloat16),
                pltpu.VMEM((cores, depth, half), jnp.bfloat16),
                pltpu.SemaphoreType.DMA((cores, parts)),
            ],
        ),
    )(which, own, other, *weights)


def pair_of(n_own, n_seq):
    fits = [p for p in range(1, n_own) if n_own % p == 0 and n_own // p * n_seq <= BLOCKS]
    return fits[0] if fits else n_own


def run(sizes, root_g, latents, policy_out, w_qkv, w_out, qk_gains, mod_table, timestep, owner):
    n_own, n_seq, n_tp = sizes
    pair = pair_of(n_own, n_seq)
    groups = n_own // pair
    root = owner[0] // w_qkv.shape[0]
    root_c = root % pair
    own, y, z = lax.axis_index("own"), lax.axis_index("seq"), lax.axis_index("tp")
    group, core = own // pair, own % pair
    both = ("own", "seq")

    def at(g, c, s):
        return ((g + root_g) % groups * pair + c) * n_seq + s % n_seq

    def send(value, a, b, d):
        return lax.ppermute(value, both, [(at(a, c, s), at(b, c, s + d)) for c in range(pair) for s in range(n_seq)])

    def shift(value, dc, d=0):
        perm = [(at(g, c, s), at(g, (c + dc) % pair, s + d)) for g in range(groups) for c in range(pair) for s in range(n_seq)]
        return lax.ppermute(value, both, perm)

    def of_root_core(value):
        out = value
        for dc in range(1, pair):
            got = shift(value, dc)
            out = got if pair == 2 else jnp.where((core - dc) % pair == root_c, got, out)
        return out

    stored = owner[0] % w_qkv.shape[0]
    rows, width = latents.shape[1:]
    cols = w_qkv.shape[3]
    heads = cols // HD
    full, rest = heads // n_seq, heads % n_seq
    share_cols = width // n_tp

    kinds_first = w_qkv.transpose(0, 2, 1, 3)
    paired = n_tp == 2 * n_seq and n_seq == 2 and groups > 1 and pair == 2 and share_cols % (pair * HD) == 0
    ints = [timestep[0], y, stored]
    if paired:
        half = share_cols // pair
        keep, give = z % 2 * share_cols, (1 - z % 2) * share_cols
        ints += [keep + core * half, give + core * half, keep + (1 - core) * half, give + (1 - core) * half]
    pieces, mine, mine_out = prepare(
        latents[0], mod_table.transpose(1, 0, 2), kinds_first, w_out, jnp.stack(ints), n_seq, half if paired else HD
    )
    blocks = {(0, 0): pieces[0]}
    for dg in range(1, groups):
        blocks[dg, 0] = send(pieces[0], dg, 0, 0)
    for d in range(1, n_seq):
        blocks[0, d] = lax.ppermute(pieces[d], "seq", [(s, (s + d) % n_seq) for s in range(n_seq)])

    mine_gains = lax.dynamic_index_in_dim(qk_gains, stored, 0, keepdims=False)

    got_weights = of_root_core(mine)
    gains = jnp.where(core == root_c, mine_gains, of_root_core(mine_gains))
    gains = gains.astype(jnp.float32).reshape(2, heads, HD)
    gains = jnp.concatenate([lax.dynamic_slice_in_dim(gains, full * y, full, 1), gains[:, full * n_seq :]], 1)
    ints = jnp.stack([(own == root).astype(jnp.int32), stored, y])

    far_near, far_far, hops = [], [], []
    early = sorted(blocks)
    late = [(dg, d) for dg in range(1, groups) for d in range(1, n_seq)]
    chunks = [[key] for key in early + late]
    own_part, other_part, arrivals = {}, {}, []
    previous = None
    for number, chunk in enumerate(chunks):
        queries = [[(d + dd) % n_seq == 0 for dd in range(n_seq)] for _, d in chunk]
        x = [blocks[key] for key in chunk]
        if previous is not None:
            x[0] = after(x[0], previous)
        if number == 0:
            x[0] = after(x[0], gains)
        if number == len(chunks) - 1:
            x[0] = after(x[0], *arrivals[: -n_seq + 1])
        parts = project(x, kinds_first, got_weights, ints, full, rest, queries)
        previous = parts[0]
        base = 0
        for key, q in zip(chunk, queries):
            own_part[key] = (parts[0], base)
            base += unit_count(full, rest, q[0])
        for dd in range(1, n_seq):
            got = send(after(parts[dd], *arrivals[-1:]) if 0 < number < len(chunks) - 1 else parts[dd], 0, 0, dd)
            arrivals.append(got)
            base = 0
            for (dg, d), q in zip(chunk, queries):
                other_part.setdefault((dg, (d + dd) % n_seq), []).append((got, base))
                base += unit_count(full, rest, q[dd])
        if number == 0:
            for dg, d in late:
                blocks[dg, d] = send(after(blocks[0, d], previous, blocks[dg, 0]), dg, 0, 0)
        if number == 0 and paired:
            got = after(shift(mine_out[2:], 1), previous)
            here = jnp.where(core == root_c, mine_out[:2], got)
            taken = lax.ppermute(here[1], "tp", [(t, t ^ 1) for t in range(n_tp)])
            near = [here[0], taken]
            far_near = [[send(here[0], 0, dg, 0)] for dg in range(1, groups)]
        if paired and number == 2:
            for dg in range(1, groups):
                far_near[dg - 1].append(send(after(near[1], own_part[chunks[1][0]][0]), 0, dg, 0))
            far_far = [[send(values[0], dg + 1, dg + 1, 1)] for dg, values in enumerate(far_near)]
    last = previous

    def chosen(here, there, first):
        out = jnp.concatenate([after(value, first) for value in here], 0)
        for dg in range(1, groups):
            values = jnp.concatenate([after(value, first) for value in there[dg - 1]], 0)
            out = jnp.where(group == (root_g + dg) % groups, values, out)
        return [out, shift(out, 1)]

    if paired:
        for dg, values in enumerate(far_near):
            far_far[dg].append(send(after(values[1], last), dg + 1, dg + 1, 1))
        back = [send(far_far[0][0], 1, 0, 0)]
        near_w = chosen(near, far_near, last)
    combined, all_kv = [], [[] for _ in range(pair)]
    order = sorted(blocks)
    hops = [near_w[0], *[values[0] for values in far_far], arrivals[-2]] if paired else []
    for keys in [order[i : i + 2] for i in range(0, len(order), 2)]:
        combined.append(
            combine(
                [own_part[key] for key in keys],
                [other_part.get(key, []) for key in keys],
                after(gains, last, *hops),
                full,
                rest,
                [d == 0 for _, d in keys],
            )
        )
        for dc in range(pair):
            value = combined[-1][1]
            all_kv[dc].append(shift(value, dc) if dc else value)
        hops = [values[-1] for values in all_kv] + (back if paired else [])
    last = combined[-1][2]
    if paired:
        back.append(send(far_far[0][1], 1, 0, 0))
        hops = [back[0], *[values[1] for values in far_far]]

    sums = jnp.concatenate([part[2] for part in combined], 1)
    parts = [sums]
    for d in range(1, n_tp):
        parts.append(lax.ppermute(sums, "tp", [(t, (t + d) % n_tp) for t in range(n_tp)]))
    sums = sum(parts[1:], parts[0])

    all_sums = [[shift(sums, dc, d) if dc or d else sums for d in range(n_seq)] for dc in range(pair)]

    arrived, results = {}, []
    for key in sorted(order, key=lambda key: (-key[0], key[1] if key[0] else -key[1])):
        query = combined[order.index(key) // 2][0][order.index(key) % 2]
        if query is None:
            continue
        if arrived:
            query = after(query, previous)
        elif paired:
            query = after(query, *hops)
        if key == (0, 0):
            query = after(query, *[arrived[k] for k in arrived if k[0]])
        result = attend(order.index(key), query, all_kv, all_sums, cols * n_tp, full + rest)
        previous = result
        results.append(result)
        if paired and len(results) == 2:
            far_w = chosen(back, far_far, previous)
        dg, d = key
        arrived[key] = send(result, 0, dg, -d) if key != (0, 0) else result
    from_seq = []
    at_rest = None
    for d in range(n_seq):
        if (0, d) not in arrived:
            continue
        here = arrived[0, d]
        for dg in range(1, groups):
            here = jnp.where(group == (root_g + dg) % groups, arrived[dg, d], here)
        from_seq.append(here[:full])
        if d == 0:
            at_rest = here[full:]
    turn = (jnp.arange(n_seq) - y) % n_seq
    if full:
        if n_seq == 2:
            ordered = jnp.concatenate(
                [jnp.where(y == 0, from_seq[0], from_seq[1]), jnp.where(y == 0, from_seq[1], from_seq[0]), at_rest], 0
            )
        else:
            ordered = jnp.take(jnp.stack(from_seq), turn, axis=0).reshape(n_seq * full, rows, HD)
            ordered = jnp.concatenate([ordered, at_rest], 0)
    else:
        ordered = at_rest

    if paired:
        out_weights = near_w + far_w
        other = lax.ppermute(ordered, "tp", [(t, t ^ 1) for t in range(n_tp)])
        mine_first = (y == z // 2).astype(jnp.int32)
        sent = output(jnp.stack([mine_first, core]), ordered, other, out_weights, jnp.bfloat16)
        got = lax.ppermute(sent, "tp", [(t, (t + 2) % n_tp) for t in range(n_tp)])
        kept = output(jnp.stack([1 - mine_first, core]), ordered, after(other, sent), out_weights, jnp.float32)
        share = kept + got.astype(jnp.float32)
    else:
        attn = ordered.transpose(1, 0, 2).reshape(rows, cols)
        mine_out = lax.dynamic_index_in_dim(w_out, stored, 0, keepdims=False)
        spread_out = mine_out
        for dg in range(1, groups):
            got = send(mine_out, 0, dg, 0)
            spread_out = jnp.where(group == (root_g + dg) % groups, got, spread_out)
        parts = [spread_out]
        for d in range(1, n_seq):
            parts.append(shift(spread_out, 0, d))
        out_w = jnp.take(jnp.stack(parts), (y - jnp.arange(n_seq)) % n_seq, axis=0)
        out_w = jnp.where(core == root_c, out_w, of_root_core(out_w))
        proj = jnp.einsum("tk,skn->tsn", attn, out_w, preferred_element_type=jnp.float32)
        proj = proj.reshape(rows, n_tp, share_cols).transpose(1, 0, 2)
        sent = proj.astype(jnp.bfloat16)
        share = lax.dynamic_index_in_dim(proj, z, 0, keepdims=False)
        for d in range(1, n_tp):
            piece = lax.dynamic_index_in_dim(sent, (z + d) % n_tp, 0, keepdims=False)
            got = lax.ppermute(piece, "tp", [(t, (t + d) % n_tp) for t in range(n_tp)])
            share = share + got.astype(jnp.float32)
    inputs = lax.dynamic_slice_in_dim(latents[0], z * share_cols, share_cols, 1).astype(jnp.float32)
    gate = lax.dynamic_slice(mod_table, (timestep[0], 2, z * share_cols), (1, 1, share_cols))[0]
    block = (inputs + gate * share).astype(jnp.bfloat16)
    differ = block.astype(jnp.float32) - policy_out[0].astype(jnp.float32)
    squares = jnp.sum(differ * differ, axis=-1)
    parts = [squares]
    for d in range(1, n_tp):
        parts.append(lax.ppermute(squares, "tp", [(t, (t + d) % n_tp) for t in range(n_tp)]))
    squares = sum(parts[1:], parts[0]) / width
    return lax.optimization_barrier((block[None], squares[None]))


def local(sizes, *args):
    w_qkv, owner = args[2], args[7]
    pair = pair_of(*sizes[:2])
    branches = [functools.partial(run, sizes, g) for g in range(sizes[0] // pair)]
    return lax.switch(owner[0] // w_qkv.shape[0] // pair, branches, *args)


def solution(mesh):
    placed = (
        P(None, ("own", "seq"), None),
        P(None, ("own", "seq"), "tp"),
        P("own", "seq", None, "tp"),
        P("own", "tp", "seq"),
        P("own", None, "tp"),
        P(),
        P(),
        P(),
    )
    sizes = tuple(mesh.shape[axis] for axis in ("own", "seq", "tp"))
    return jax.shard_map(
        functools.partial(local, sizes),
        mesh=mesh,
        in_specs=placed,
        out_specs=(P(None, ("own", "seq"), "tp"), P(None, ("own", "seq"))),
        check_vma=False,
    )
```
